32 devices in a mesh: grp: 2 (over x), node: 16 (over z, y, core).
Axes of the slice: x: 2, y: 2, z: 4, core: 2. Of those that a mesh axis runs over, the one named last changes fastest.
Arguments:
- nodes: bfloat16 [128, 2, 1024, 1024], P('grp', None, 'node'), parts along dimension 0, may hold values from -0.34960938 to 0.34960938
- pair_nodes: int32 [16, 2], replicated, may hold values from 0 to 63
- prod_left: int32 [16], replicated, may hold values from 0 to 15, as said below
- prod_right: int32 [16], replicated, may hold values from 0 to 15, each once
- prod_flag: int32 [16], replicated, may hold values from 0 to 1
- prod_diag: int32 [16], replicated, may hold values from 0 to 7, as said below
Outputs:
- diagrams: bfloat16 [16, 2, 1024, 1024], P('grp', None, 'node'), parts along dimension 0
The draws below stay inside these ranges and needn't reach their ends.
There are 2 independent parts, one for each index of `grp`. The reference program is written for one: setup_inputs(seed, part) draws one part's arguments, and reference() takes and returns one part's arrays. A program takes and returns all parts, laid end to end along the dimension named above; an argument that names none is the same for every part. Nothing has to cross between parts.
Inputs may be any that keep to these rules, and one draw needn't show every extreme that they name: `prod_left`: exactly 8 distinct pairs are left operands, each of exactly two products. `prod_diag`: every diagram receives exactly two products.
All inputs are finite; a program needn't handle non-finite values.
Results may differ from the reference program's by a relative error of at most 0.0065.
Values may be sent and summed in bfloat16 or wider, within the bound.
No kernel may reach another device: no remote copies, remote signals or barrier semaphores. Data moves between devices by JAX's collectives and lax.ppermute only.
A program may use at most 128 MiB of HBM per device.

```python
import jax
import jax.numpy as jnp
from jax import lax

M = 1024
NODES = 64
PAIRS = 16
PRODS = 16
DIAGS = 8


def draw_prod_left(key, part):
    base = jax.random.permutation(jax.random.fold_in(key, 11), PAIRS).astype(jnp.int32)
    return base[jnp.arange(PRODS, dtype=jnp.int32) // 2].astype(jnp.int32)


def draw_prod_diag(key, part):
    order = jax.random.permutation(jax.random.fold_in(key, 23), PRODS).astype(jnp.int32)
    return (order % DIAGS).astype(jnp.int32)


def plant(result, key, low, top_value):
    longest = result.shape.index(max(result.shape))
    spots = []
    for shift in (0, 1):
        where = [jax.random.randint(jax.random.fold_in(key, axis), (), 0, length) for axis, length in enumerate(result.shape)]
        where[longest] = (where[longest] + shift) % result.shape[longest]
        spots.append(tuple(where))
    return result.at[spots[0]].set(low).at[spots[1]].set(top_value)


def steps_of(stream_key, shape, shards, low, top_value):
    gain = 1.0
    for position, blocks in shards:
        draws = jax.random.uniform(jax.random.fold_in(jax.random.fold_in(stream_key, 6), position), (blocks,), jnp.float32, low / len(shards), top_value / len(shards))
        gain = gain * jnp.repeat(jnp.exp(draws), shape[position] // blocks).reshape((-1,) + (1,) * (len(shape) - 1 - position))
    return gain


def noise(own_key, shape, spread, bound, pieces=(), held_as=jnp.bfloat16):
    array = spread * jax.random.normal(own_key, shape, jnp.float32)
    if pieces:
        array = array * steps_of(own_key, shape, pieces, -0.22, 0.18)
    return jnp.clip(array, -bound, bound).astype(held_as)


def setup_inputs(seed: int = 0, part: int = 0) -> dict:
    keys = jax.random.split(jax.random.key(seed), 7)
    own_keys = jax.random.split(jax.random.fold_in(keys[6], part), 7)
    return {
        "nodes": noise(own_keys[0], (NODES, 2, M, M), 0.0573, 0.34960938, ((2, 16),)),
        "pair_nodes": plant(jax.random.randint(keys[1], (PAIRS, 2), 0, NODES), jax.random.fold_in(keys[1], 1), 0, NODES - 1).astype(jnp.int32),
        "prod_left": draw_prod_left(jax.random.fold_in(keys[6], 71), part),
        "prod_right": jax.random.permutation(keys[3], PAIRS).astype(jnp.int32),
        "prod_flag": plant(jax.random.randint(keys[4], (PRODS,), 0, 2), jax.random.fold_in(keys[4], 1), 0, 1).astype(jnp.int32),
        "prod_diag": draw_prod_diag(jax.random.fold_in(keys[6], 71), part),
    }


def complex_product(left_re, left_im, right_re, right_im):
    real_part = jnp.dot(left_re, right_re, preferred_element_type=jnp.float32) - jnp.dot(left_im, right_im, preferred_element_type=jnp.float32)
    imag_part = jnp.dot(left_re, right_im, preferred_element_type=jnp.float32) + jnp.dot(left_im, right_re, preferred_element_type=jnp.float32)
    return jnp.stack([real_part, imag_part]).astype(jnp.bfloat16)


def reference(nodes, pair_nodes, prod_left, prod_right, prod_flag, prod_diag):
    def pair_one(entry):
        left_node = nodes[entry[0]]
        right_node = nodes[entry[1]]
        return complex_product(left_node[0], left_node[1], right_node[0], right_node[1])

    paired = lax.map(pair_one, pair_nodes)

    def second_one(entry):
        left_pair = paired[entry[0]]
        right_pair = paired[entry[1]]
        flipped = entry[2] == 1
        left_re = jnp.where(flipped, left_pair[0].T, left_pair[0])
        left_im = jnp.where(flipped, -left_pair[1].T, left_pair[1])
        return complex_product(left_re, left_im, right_pair[0], right_pair[1])

    entries = jnp.stack([prod_left, prod_right, prod_flag], axis=1)
    results = lax.map(second_one, entries)
    diagram_map = (prod_diag[None, :] == jnp.arange(DIAGS, dtype=jnp.int32)[:, None]).astype(jnp.float32)
    summed = jnp.dot(diagram_map, results.reshape(PRODS, -1).astype(jnp.float32), precision=lax.Precision.HIGHEST)
    return summed.reshape(DIAGS, 2, M, M).astype(jnp.bfloat16)
```

```python
import functools

import jax
import jax.numpy as jnp
from jax import lax
from jax.experimental import pallas as pl
from jax.experimental.pallas import tpu as pltpu
from jax.sharding import PartitionSpec as P

PARTS = 2
VMEM_BYTES = 48 * 1024 * 1024
SMEM = pl.BlockSpec(memory_space=pltpu.SMEM)
HBM = pl.BlockSpec(memory_space=pl.ANY)
VMEM = pl.BlockSpec(memory_space=pltpu.VMEM)


def params():
    return pltpu.CompilerParams(vmem_limit_bytes=VMEM_BYTES)


def route_kernel(prods, pair_nodes, prod_left, prod_right, prod_flag, prod_diag, table):
    half = prods // 2

    def clear(d, carry):
        table[5, d] = -1
        return carry

    lax.fori_loop(0, prods, clear, 0)

    def rank(k, carry):
        mine = prod_left[k]

        def count(j, total):
            other = prod_left[j]
            before = jnp.logical_or(other < mine, jnp.logical_and(other == mine, j < k))
            return total + before.astype(jnp.int32)

        place = lax.fori_loop(0, prods, count, 0, unroll=True)
        right = prod_right[k]
        table[0, place] = pair_nodes[mine, lax.rem(place, 2)]
        table[1, place] = pair_nodes[right, 0]
        table[2, place] = pair_nodes[right, 1]
        table[3, place] = prod_flag[k]
        table[4, place] = prod_diag[k]
        return carry

    lax.fori_loop(0, prods, rank, 0)

    def diagram(place, carry):
        d = table[4, place]
        second = (table[5, d] >= 0).astype(jnp.int32)
        table[5, d + second * half] = place
        return carry

    lax.fori_loop(0, prods, diagram, 0)


def route(pair_nodes, prod_left, prod_right, prod_flag, prod_diag):
    prods = prod_left.shape[0]
    return pl.pallas_call(
        functools.partial(route_kernel, prods),
        out_shape=jax.ShapeDtypeStruct((8, prods), jnp.int32),
        in_specs=[SMEM] * 5,
        out_specs=SMEM,
        name="route",
    )(pair_nodes, prod_left, prod_right, prod_flag, prod_diag)


def pick_kernel(table, node, out):
    out[...] = node[...]


def pick(table, nodes, row, part, width):
    count = table.shape[1]
    block = (1, nodes.shape[1], nodes.shape[2], width)
    return pl.pallas_call(
        pick_kernel,
        out_shape=jax.ShapeDtypeStruct((count,) + block[1:], nodes.dtype),
        grid_spec=pltpu.PrefetchScalarGridSpec(
            num_scalar_prefetch=1,
            grid=(count,),
            in_specs=[pl.BlockSpec(block, lambda t, table: (table[row, t], 0, 0, part))],
            out_specs=pl.BlockSpec(block, lambda t, table: (t, 0, 0, 0)),
        ),
        cost_estimate=pl.CostEstimate(
            flops=0, transcendentals=0, bytes_accessed=4 * count * block[1] * block[2] * width
        ),
        name="pick",
    )(table, nodes)


def dot(a, b):
    return jnp.dot(a, b, preferred_element_type=jnp.float32)


def left_kernel(table, place, own, other, out, left, right, sems):
    order = left.shape[2] * left.shape[0]
    core = lax.rem(place[0], 2)
    flag = table[3, place[0]]

    def load(first, second):
        one = pltpu.make_async_copy(first, left, sems.at[0])
        two = pltpu.make_async_copy(second, right, sems.at[1])
        one.start()
        two.start()
        one.wait()
        two.wait()

    @pl.when(core == 0)
    def _():
        load(own, other)

    @pl.when(core == 1)
    def _():
        load(other, own)

    b_re = right[:, 0].reshape(order, order)
    b_im = right[:, 1].reshape(order, order)
    step = order // 4
    per = left.shape[0] // 4
    for block in range(4):
        a_re = left[block * per : (block + 1) * per, 0].reshape(step, order)
        a_im = left[block * per : (block + 1) * per, 1].reshape(step, order)
        re = (dot(a_re, b_re) - dot(a_im, b_im)).astype(out.dtype)
        im = (dot(a_re, b_im) + dot(a_im, b_re)).astype(out.dtype)

        @pl.when(flag == 0)
        def _():
            out[0, block * step : (block + 1) * step, :] = re
            out[1, block * step : (block + 1) * step, :] = im

        @pl.when(flag == 1)
        def _():
            out[0, :, block * step : (block + 1) * step] = re.T
            out[1, :, block * step : (block + 1) * step] = -im.T


def left_pair(table, place, own, other):
    order = own.shape[3]
    return pl.pallas_call(
        left_kernel,
        out_shape=jax.ShapeDtypeStruct((2, order, order), own.dtype),
        in_specs=[SMEM, SMEM, HBM, HBM],
        out_specs=VMEM,
        scratch_shapes=[
            pltpu.VMEM(own.shape, own.dtype),
            pltpu.VMEM(own.shape, own.dtype),
            pltpu.SemaphoreType.DMA((2,)),
        ],
        compiler_params=params(),
        cost_estimate=pl.CostEstimate(
            flops=8 * order**3, transcendentals=0, bytes_accessed=12 * order * order
        ),
        name="left_pair",
    )(table, place, own, other)


def product_kernel(left, right, out):
    order = left.shape[2]
    width = right.shape[3]
    b_re = right[:, 0].reshape(order, width)
    b_im = right[:, 1].reshape(order, width)
    step = order // 4
    panels = len(out.shape) == 4
    for block in range(4):
        rows = slice(block * step, (block + 1) * step)
        a_re = left[0, rows, :]
        a_im = left[1, rows, :]
        re = (dot(a_re, b_re) - dot(a_im, b_im)).astype(out.dtype)
        im = (dot(a_re, b_im) + dot(a_im, b_re)).astype(out.dtype)
        if panels:
            per = out.shape[0] // 4
            place = slice(block * per, (block + 1) * per)
            out[place, 0] = re.reshape(per, out.shape[2], width)
            out[place, 1] = im.reshape(per, out.shape[2], width)
        else:
            out[0, rows, :] = re
            out[1, rows, :] = im


def product(left, right, panels):
    order = left.shape[2]
    width = right.shape[3]
    shape = right.shape if panels else (2, order, width)
    return pl.pallas_call(
        product_kernel,
        out_shape=jax.ShapeDtypeStruct(shape, left.dtype),
        in_specs=[VMEM, VMEM],
        out_specs=VMEM,
        compiler_params=params(),
        cost_estimate=pl.CostEstimate(
            flops=8 * order * order * width,
            transcendentals=0,
            bytes_accessed=4 * (order * order + 2 * order * width),
        ),
        name="product",
    )(left, right)


def diagrams_kernel(table, *refs):
    parts, out = refs[:-1], refs[-1]
    width = parts[0].shape[3]
    d = pl.program_id(0)
    half = table.shape[1] // 2
    one, two = table[5, d], table[5, d + half]
    for j, part in enumerate(parts):
        total = part[one].astype(jnp.float32) + part[two].astype(jnp.float32)
        out[0, :, :, j * width : (j + 1) * width] = total.astype(out.dtype)


def diagrams_of(table, parts):
    count, two, rows, width = parts[0].shape
    whole = width * len(parts)
    return pl.pallas_call(
        diagrams_kernel,
        out_shape=jax.ShapeDtypeStruct((count // 2, two, rows, whole), parts[0].dtype),
        grid=(count // 2,),
        in_specs=[SMEM] + [VMEM] * len(parts),
        out_specs=pl.BlockSpec((1, two, rows, whole), lambda d: (d, 0, 0, 0)),
        compiler_params=params(),
        name="diagrams",
    )(table, *parts)


def exchange(x):
    return lax.all_to_all(x, "node", split_axis=0, concat_axis=0, tiled=True)


def after(x, earlier):
    return lax.optimization_barrier((x, earlier))[0]


def local(size, nodes, pair_nodes, prod_left, prod_right, prod_flag, prod_diag):
    place = lax.axis_index("node").astype(jnp.int32).reshape(1)
    order = nodes.shape[3]
    width = order // PARTS
    table = route(pair_nodes, prod_left, prod_right, prod_flag, prod_diag)
    own = exchange(pick(table, nodes, 0, 0, order))
    other = lax.ppermute(own, "node", [(i, i ^ 1) for i in range(size)])
    middle = exchange(after(pick(table, nodes, 1, 0, order), own))
    left = left_pair(table, place, own, other)
    half = product(left, middle, False)
    arrived = middle
    results = []
    for j in range(PARTS):
        arrived = exchange(after(pick(table, nodes, 2, j, width), arrived))
        results.append(product(half, arrived, True))
    parts = []
    for result in results:
        arrived = exchange(after(result, arrived))
        parts.append(arrived)
    return diagrams_of(table, parts)


def solution(mesh):
    placed = (P("grp", None, "node", None), P(), P(), P(), P(), P())
    return jax.shard_map(
        functools.partial(local, mesh.shape["node"]),
        mesh=mesh,
        in_specs=placed,
        out_specs=P("grp", None, "node", None),
        check_vma=False,
    )
```

```python
import functools

import jax
import jax.numpy as jnp
from jax import lax
from jax.experimental import pallas as pl
from jax.experimental.pallas import tpu as pltpu
from jax.sharding import PartitionSpec as P

SHARES = (1, 1)
SET = 4
BLOCKS = 4
VMEM_BYTES = 48 * 1024 * 1024
SMEM = pl.BlockSpec(memory_space=pltpu.SMEM)
HBM = pl.BlockSpec(memory_space=pltpu.HBM)
VMEM = pl.BlockSpec(memory_space=pltpu.VMEM)


def params():
    return pltpu.CompilerParams(vmem_limit_bytes=VMEM_BYTES)


def route_kernel(
    prods, place_ref, pair_nodes, prod_left, prod_right, prod_flag, prod_diag, table, by_left, mate, seen, kind, slots
):
    diags = prods // 2
    mine = place_ref[0] // SET

    def clear(k, carry):
        mate[k] = 0
        seen[k] = 0
        slots[k] = 0
        table[4, k] = -1
        table[5, k] = -1
        table[6, k] = 0
        table[7, k] = -1
        table[8, k] = 0
        return carry

    lax.fori_loop(0, prods, clear, 0)

    def rank(k, carry):
        own = prod_left[k]

        def count(j, total):
            other = prod_left[j]
            before = jnp.logical_or(other < own, jnp.logical_and(other == own, j < k))
            return total + before.astype(jnp.int32)

        by_left[lax.fori_loop(0, prods, count, 0, unroll=True)] = k
        return carry

    lax.fori_loop(0, prods, rank, 0)

    def pair_up(s, carry):
        own = prod_diag[by_left[s]]

        def find(j, found):
            same = jnp.logical_and(prod_diag[by_left[j]] == own, j != s)
            return jnp.where(same, j, found)

        mate[s] = lax.fori_loop(0, prods, find, s, unroll=True)
        return carry

    lax.fori_loop(0, prods, pair_up, 0)

    def sibling_of(s):
        return s + 1 - 2 * lax.rem(s, 2)

    def kind_of(g, carry):
        def step(_, state):
            s, length = state
            back = s // 2 == g
            return jnp.where(back, s, mate[sibling_of(s)]), jnp.where(back, length, length + 1)

        _, length = lax.fori_loop(0, diags, step, (mate[2 * g + 1], 1))
        kind[g] = jnp.where(lax.rem(length, 2) == 0, 0, jnp.where(length == 1, 2, 1))
        return carry

    lax.fori_loop(0, diags, kind_of, 0)

    def add(device, s):
        k = by_left[s]
        right = prod_right[k]
        table[0, device] = pair_nodes[prod_left[k], lax.rem(device, 2)]
        table[1, device] = pair_nodes[right, 0]
        table[2, device] = pair_nodes[right, 1]
        table[3, device] = prod_flag[k]
        d = prod_diag[k]
        owner = device // SET
        code = SET * jnp.bitwise_xor(owner, mine)
        earlier = table[4, d]
        shared = jnp.logical_and(earlier >= 0, earlier // SET == code // SET)
        slot = jnp.where(shared, earlier - code, slots[owner])

        @pl.when(jnp.logical_not(shared))
        def _():
            slots[owner] = slot + 1
            table[8, 0] = jnp.maximum(table[8, 0], slot + 1)
            table[jnp.where(earlier >= 0, 5, 4), d] = code + slot

        @pl.when(owner == mine)
        def _():
            table[jnp.where(shared, 7, 6), slot] = lax.rem(device, SET)

    def walk(n, carry):
        s, last = carry

        def first(j, found):
            g = diags - 1 - j
            own = kind[g]
            worth = jnp.where(own == 0, 3, jnp.where(own == last, 1, 2))
            worth = jnp.where(seen[g] == 0, worth, 0)
            best, at = found
            return jnp.maximum(best, worth), jnp.where(worth >= best, g, at)

        _, fresh = lax.fori_loop(0, diags, first, (1, 0), unroll=True)
        s = jnp.where(seen[s // 2] == 0, s, 2 * fresh)
        seen[s // 2] = 1
        add(2 * n, s)
        add(2 * n + 1, sibling_of(s))
        return mate[sibling_of(s)], kind[s // 2]

    lax.fori_loop(0, diags, walk, (0, 2))


def route(place, pair_nodes, prod_left, prod_right, prod_flag, prod_diag):
    prods = prod_left.shape[0]
    return pl.pallas_call(
        functools.partial(route_kernel, prods),
        out_shape=jax.ShapeDtypeStruct((9, prods), jnp.int32),
        in_specs=[SMEM] * 6,
        out_specs=SMEM,
        scratch_shapes=[pltpu.SMEM((prods,), jnp.int32)] * 5,
        name="route",
    )(place, pair_nodes, prod_left, prod_right, prod_flag, prod_diag)


def pick_kernel(row, start, table, nodes, out, held, reads, writes):
    count, _, _, width = out.shape

    def read(t):
        node = nodes.at[table[row, t], :, :, pl.ds(start, width)]
        return pltpu.make_async_copy(node, held.at[t], reads.at[t])

    def write(t):
        return pltpu.make_async_copy(held.at[t], out.at[t], writes.at[t])

    for t in range(count):
        read(t).start()
    for t in range(count):
        read(t).wait()
        write(t).start()
    for t in range(count):
        write(t).wait()


def pick(table, nodes, row, start, width):
    count = table.shape[1]
    shape = (count, nodes.shape[1], nodes.shape[2], width)
    return pl.pallas_call(
        functools.partial(pick_kernel, row, start),
        out_shape=jax.ShapeDtypeStruct(shape, nodes.dtype),
        in_specs=[SMEM, HBM],
        out_specs=HBM,
        scratch_shapes=[
            pltpu.VMEM(shape, nodes.dtype),
            pltpu.SemaphoreType.DMA((count,)),
            pltpu.SemaphoreType.DMA((count,)),
        ],
        compiler_params=params(),
        name="pick",
    )(table, nodes)


def dot(a, b):
    return jnp.dot(a, b, preferred_element_type=jnp.float32)


def left_kernel(table, place, own, other, out, left, right, sems):
    order = left.shape[2] * left.shape[0]
    core = lax.rem(place[0], 2)
    flag = table[3, place[0]]

    def load(first, second):
        one = pltpu.make_async_copy(first, left, sems.at[0])
        two = pltpu.make_async_copy(second, right, sems.at[1])
        one.start()
        two.start()
        one.wait()
        two.wait()

    @pl.when(core == 0)
    def _():
        load(own, other)

    @pl.when(core == 1)
    def _():
        load(other, own)

    b_re = right[:, 0].reshape(order, order)
    b_im = right[:, 1].reshape(order, order)
    step = order // 4
    per = left.shape[0] // 4
    for block in range(4):
        a_re = left[block * per : (block + 1) * per, 0].reshape(step, order)
        a_im = left[block * per : (block + 1) * per, 1].reshape(step, order)
        re = (dot(a_re, b_re) - dot(a_im, b_im)).astype(out.dtype)
        im = (dot(a_re, b_im) + dot(a_im, b_re)).astype(out.dtype)

        @pl.when(flag == 0)
        def _():
            out[0, block * step : (block + 1) * step, :] = re
            out[1, block * step : (block + 1) * step, :] = im

        @pl.when(flag == 1)
        def _():
            out[0, :, block * step : (block + 1) * step] = re.T
            out[1, :, block * step : (block + 1) * step] = -im.T


def left_pair(table, place, own, other):
    order = other.shape[3]
    return pl.pallas_call(
        left_kernel,
        out_shape=jax.ShapeDtypeStruct((2, order, order), own.dtype),
        in_specs=[SMEM, SMEM, HBM, HBM],
        out_specs=VMEM,
        scratch_shapes=[
            pltpu.VMEM(other.shape, other.dtype),
            pltpu.VMEM(other.shape, other.dtype),
            pltpu.SemaphoreType.DMA((2,)),
        ],
        compiler_params=params(),
        name="left_pair",
    )(table, place, own, other)


def product_kernel(left, right, out):
    order = left.shape[2]
    b_re = right[:, 0].reshape(order, order)
    b_im = right[:, 1].reshape(order, order)
    step = order // BLOCKS
    for block in range(BLOCKS):
        rows = slice(block * step, (block + 1) * step)
        a_re = left[0, rows, :]
        a_im = left[1, rows, :]
        out[0, rows, :] = (dot(a_re, b_re) - dot(a_im, b_im)).astype(out.dtype)
        out[1, rows, :] = (dot(a_re, b_im) + dot(a_im, b_re)).astype(out.dtype)


def product(left, right):
    order = left.shape[2]
    return pl.pallas_call(
        product_kernel,
        out_shape=jax.ShapeDtypeStruct(left.shape, left.dtype),
        in_specs=[VMEM, VMEM],
        out_specs=VMEM,
        compiler_params=params(),
        name="product",
    )(left, right)


def panels_kernel(place, left, right, *refs):
    outs, scratch = refs[:-1], refs[-1]
    order = left.shape[2]
    width = right.shape[3]
    rows_each = right.shape[2]
    b_re = right[:, 0].reshape(order, width)
    b_im = right[:, 1].reshape(order, width)
    step = order // BLOCKS
    per = step // rows_each
    own = lax.rem(place[0], SET)
    for block in range(BLOCKS):
        rows = slice(block * step, (block + 1) * step)
        a_re = left[0, rows, :]
        a_im = left[1, rows, :]
        re = (dot(a_re, b_re) - dot(a_im, b_im)).astype(scratch.dtype)
        im = (dot(a_re, b_im) + dot(a_im, b_re)).astype(scratch.dtype)
        panels = slice(block * per, (block + 1) * per)
        scratch[panels, 0] = re.reshape(per, rows_each, width)
        scratch[panels, 1] = im.reshape(per, rows_each, width)
    for s, out in enumerate(outs):
        target = jnp.bitwise_xor(own, s)
        for owner in range(out.shape[0]):
            out[owner] = scratch[SET * owner + target]


def panels_of(place, left, right):
    order = left.shape[2]
    count, two, rows, width = right.shape
    return pl.pallas_call(
        panels_kernel,
        out_shape=[jax.ShapeDtypeStruct((count // SET, two, rows, width), left.dtype)] * SET,
        in_specs=[SMEM, VMEM, VMEM],
        out_specs=[VMEM] * SET,
        scratch_shapes=[pltpu.VMEM(right.shape, right.dtype)],
        compiler_params=params(),
        name="panels",
    )(place, left, right)


def partial_kernel(table, place, *refs):
    pieces, outs, scratch = refs[:SET], refs[SET:-1], refs[-1]
    own = lax.rem(place[0], SET)
    mine = place[0] // SET
    for s, piece in enumerate(pieces):
        scratch[s] = piece[...]
    for slot in range(outs[0].shape[0]):
        one = jnp.bitwise_xor(table[6, slot], own)
        second = table[7, slot]
        two = jnp.bitwise_xor(jnp.maximum(second, 0), own)
        for e, out in enumerate(outs):
            owner = jnp.bitwise_xor(mine, e)
            other = scratch[two, owner].astype(jnp.float32)
            total = scratch[one, owner].astype(jnp.float32) + jnp.where(second >= 0, other, 0.0)
            out[slot] = total.astype(out.dtype)


def partial_sums(slots, table, place, pieces):
    sets = pieces[0].shape[0]
    shape = pieces[0].shape[1:]
    return pl.pallas_call(
        partial_kernel,
        out_shape=[jax.ShapeDtypeStruct((slots,) + shape, pieces[0].dtype)] * sets,
        in_specs=[SMEM, SMEM] + [VMEM] * SET,
        out_specs=[VMEM] * sets,
        scratch_shapes=[pltpu.VMEM((SET,) + pieces[0].shape, pieces[0].dtype)],
        compiler_params=params(),
        name="partial_sums",
    )(table, place, *pieces)


def diagrams_kernel(parts, sets, table, *refs):
    ins, out, held = refs[: parts * sets], refs[parts * sets], refs[parts * sets + 1]

    start = 0
    for j in range(parts):
        width = ins[j * sets].shape[3]
        for e in range(sets):
            held[e, :, :, :, start : start + width] = ins[j * sets + e][...]
        start += width

    for d in range(out.shape[0]):
        one, two = table[4, d], jnp.maximum(table[5, d], 0)
        first = held[one // SET, lax.rem(one, SET)].astype(jnp.float32)
        second = held[two // SET, lax.rem(two, SET)].astype(jnp.float32)
        out[d] = (first + jnp.where(table[5, d] >= 0, second, 0.0)).astype(out.dtype)


def diagrams_of(table, parts):
    slots, two, rows, _ = parts[0][0].shape
    sets = len(parts[0])
    diags = table.shape[1] // 2
    whole = sum(pieces[0].shape[3] for pieces in parts)
    dtype = parts[0][0].dtype
    return pl.pallas_call(
        functools.partial(diagrams_kernel, len(parts), sets),
        out_shape=jax.ShapeDtypeStruct((diags, two, rows, whole), dtype),
        in_specs=[SMEM] + [VMEM] * (sets * len(parts)),
        out_specs=VMEM,
        scratch_shapes=[pltpu.VMEM((sets, slots, two, rows, whole), dtype)],
        compiler_params=params(),
        name="diagrams",
    )(table, *[x for pieces in parts for x in pieces])


def exchange(x):
    return lax.all_to_all(x, "node", split_axis=0, concat_axis=0, tiled=True)


def after(x, earlier):
    return lax.optimization_barrier((x, earlier))[0]


def swap(x, size, shift):
    return lax.ppermute(x, "node", [(i, i ^ shift) for i in range(size)])


def tail(slots, size, table, place, picks, left, middle):
    left_middle = product(left, middle)
    done = middle
    parts = []
    for picked in picks:
        last = exchange(after(picked, done))
        if parts:
            last = after(last, parts[-1][0])
        sent = panels_of(place, left_middle, last)
        pieces = [sent[0]] + [swap(sent[s], size, s) for s in range(1, SET)]
        sums = partial_sums(slots, table, place, pieces)
        done = (last, left_middle)
        parts.append([sums[0]] + [swap(x, size, SET * e) for e, x in enumerate(sums) if e])
    return diagrams_of(table, parts)


def local(size, nodes, pair_nodes, prod_left, prod_right, prod_flag, prod_diag):
    place = lax.axis_index("node").astype(jnp.int32).reshape(1)
    order = nodes.shape[3]
    table = route(place, pair_nodes, prod_left, prod_right, prod_flag, prod_diag)
    own = exchange(pick(table, nodes, 0, 0, order))
    other = swap(own, size, 1)
    middle = exchange(after(pick(table, nodes, 1, 0, order), own))
    left = left_pair(table, place, own, other)
    widths = [order * share // sum(SHARES) for share in SHARES]
    picks = [pick(table, nodes, 2, sum(widths[:j]), width) for j, width in enumerate(widths)]
    few = functools.partial(tail, SET - 1, size)
    many = functools.partial(tail, SET, size)
    return lax.cond(table[8, 0] < SET, few, many, table, place, picks, left, middle)


def solution(mesh):
    placed = (P("grp", None, "node", None), P(), P(), P(), P(), P())
    return jax.shard_map(
        functools.partial(local, mesh.shape["node"]),
        mesh=mesh,
        in_specs=placed,
        out_specs=P("grp", None, "node", None),
        check_vma=False,
    )
```

```python
import functools

import jax
import jax.numpy as jnp
from jax import lax
from jax.experimental import pallas as pl
from jax.experimental.pallas import tpu as pltpu
from jax.sharding import PartitionSpec as P

SHARES = (1, 1)
SET = 4
BLOCKS = 4
VMEM_BYTES = 48 * 1024 * 1024
PANELS_VMEM_BYTES = 56 * 1024 * 1024
WHOLE_VMEM_BYTES = 60 * 1024 * 1024
SMEM = pl.BlockSpec(memory_space=pltpu.SMEM)
HBM = pl.BlockSpec(memory_space=pltpu.HBM)
VMEM = pl.BlockSpec(memory_space=pltpu.VMEM)


def params(limit=VMEM_BYTES):
    return pltpu.CompilerParams(vmem_limit_bytes=limit)


def route_kernel(
    prods, place_ref, pair_nodes, prod_left, prod_right, prod_flag, prod_diag, table, by_left, diag, mate, seen, kind, slots
):
    diags = prods // 2
    mine = place_ref[0] // SET

    def clear(k, carry):
        mate[k] = 0
        seen[k] = 0
        slots[k] = 0
        table[4, k] = -1
        table[5, k] = -1
        table[6, k] = 0
        table[7, k] = -1
        table[8, k] = 0
        return carry

    lax.fori_loop(0, prods, clear, 0)

    def rank(k, carry):
        own = prod_left[k]

        def count(j, total):
            other = prod_left[j]
            before = jnp.logical_or(other < own, jnp.logical_and(other == own, j < k))
            return total + before.astype(jnp.int32)

        at = lax.fori_loop(0, prods, count, 0, unroll=True)
        by_left[at] = k
        diag[at] = prod_diag[k]
        return carry

    lax.fori_loop(0, prods, rank, 0)

    def pair_up(s, carry):
        own = diag[s]

        def find(j, found):
            same = jnp.logical_and(diag[j] == own, j != s)
            return jnp.where(same, j, found)

        mate[s] = lax.fori_loop(0, prods, find, s, unroll=True)
        return carry

    lax.fori_loop(0, prods, pair_up, 0)

    def sibling_of(s):
        return s + 1 - 2 * lax.rem(s, 2)

    def kind_of(g, carry):
        def step(_, state):
            s, length = state
            back = s // 2 == g
            return jnp.where(back, s, mate[sibling_of(s)]), jnp.where(back, length, length + 1)

        _, length = lax.fori_loop(0, diags, step, (mate[2 * g + 1], 1))
        kind[g] = jnp.where(lax.rem(length, 2) == 0, 0, jnp.where(length == 1, 2, 1))
        return carry

    lax.fori_loop(0, diags, kind_of, 0)

    def add(device, s):
        k = by_left[s]
        right = prod_right[k]
        table[0, device] = pair_nodes[prod_left[k], lax.rem(device, 2)]
        table[1, device] = pair_nodes[right, 0]
        table[2, device] = pair_nodes[right, 1]
        table[3, device] = prod_flag[k]
        d = diag[s]
        owner = device // SET
        code = SET * jnp.bitwise_xor(owner, mine)
        earlier = table[4, d]
        shared = jnp.logical_and(earlier >= 0, earlier // SET == code // SET)
        slot = jnp.where(shared, earlier - code, slots[owner])

        @pl.when(jnp.logical_not(shared))
        def _():
            slots[owner] = slot + 1
            table[8, 0] = jnp.maximum(table[8, 0], slot + 1)
            table[jnp.where(earlier >= 0, 5, 4), d] = code + slot

        @pl.when(owner == mine)
        def _():
            table[jnp.where(shared, 7, 6), slot] = lax.rem(device, SET)

    def walk(n, carry):
        s, last = carry

        def first(j, found):
            g = diags - 1 - j
            own = kind[g]
            worth = jnp.where(own == 0, 3, jnp.where(own == last, 1, 2))
            worth = jnp.where(seen[g] == 0, worth, 0)
            best, at = found
            return jnp.maximum(best, worth), jnp.where(worth >= best, g, at)

        _, fresh = lax.fori_loop(0, diags, first, (1, 0), unroll=True)
        s = jnp.where(seen[s // 2] == 0, s, 2 * fresh)
        seen[s // 2] = 1
        add(2 * n, s)
        add(2 * n + 1, sibling_of(s))
        return mate[sibling_of(s)], kind[s // 2]

    lax.fori_loop(0, diags, walk, (0, 2))


def route(place, pair_nodes, prod_left, prod_right, prod_flag, prod_diag):
    prods = prod_left.shape[0]
    return pl.pallas_call(
        functools.partial(route_kernel, prods),
        out_shape=jax.ShapeDtypeStruct((9, prods), jnp.int32),
        in_specs=[SMEM] * 6,
        out_specs=SMEM,
        scratch_shapes=[pltpu.SMEM((prods,), jnp.int32)] * 6,
        name="route",
    )(place, pair_nodes, prod_left, prod_right, prod_flag, prod_diag)


def pick_kernel(row, start, table, nodes, out, held, reads, writes):
    count, _, _, width = out.shape

    def read(t):
        node = nodes.at[table[row, t], :, :, pl.ds(start, width)]
        return pltpu.make_async_copy(node, held.at[t], reads.at[t])

    def write(t):
        return pltpu.make_async_copy(held.at[t], out.at[t], writes.at[t])

    for t in range(count):
        read(t).start()
    for t in range(count):
        read(t).wait()
        write(t).start()
    for t in range(count):
        write(t).wait()


def pick(table, nodes, row, start, width):
    count = table.shape[1]
    shape = (count, nodes.shape[1], nodes.shape[2], width)
    return pl.pallas_call(
        functools.partial(pick_kernel, row, start),
        out_shape=jax.ShapeDtypeStruct(shape, nodes.dtype),
        in_specs=[SMEM, HBM],
        out_specs=HBM,
        scratch_shapes=[
            pltpu.VMEM(shape, nodes.dtype),
            pltpu.SemaphoreType.DMA((count,)),
            pltpu.SemaphoreType.DMA((count,)),
        ],
        compiler_params=params(WHOLE_VMEM_BYTES),
        name="pick",
    )(table, nodes)


def dot(a, b):
    return jnp.dot(a, b, preferred_element_type=jnp.float32)


def left_kernel(table, place, own, other, out, left, right, sems):
    order = left.shape[2] * left.shape[0]
    core = lax.rem(place[0], 2)
    flag = table[3, place[0]]

    def load(first, second):
        one = pltpu.make_async_copy(first, left, sems.at[0])
        two = pltpu.make_async_copy(second, right, sems.at[1])
        one.start()
        two.start()
        one.wait()
        two.wait()

    @pl.when(core == 0)
    def _():
        load(own, other)

    @pl.when(core == 1)
    def _():
        load(other, own)

    b_re = right[:, 0].reshape(order, order)
    b_im = right[:, 1].reshape(order, order)
    step = order // 4
    per = left.shape[0] // 4
    for block in range(4):
        a_re = left[block * per : (block + 1) * per, 0].reshape(step, order)
        a_im = left[block * per : (block + 1) * per, 1].reshape(step, order)
        re = (dot(a_re, b_re) - dot(a_im, b_im)).astype(out.dtype)
        im = (dot(a_re, b_im) + dot(a_im, b_re)).astype(out.dtype)

        @pl.when(flag == 0)
        def _():
            out[0, block * step : (block + 1) * step, :] = re
            out[1, block * step : (block + 1) * step, :] = im

        @pl.when(flag == 1)
        def _():
            out[0, :, block * step : (block + 1) * step] = re.T
            out[1, :, block * step : (block + 1) * step] = -im.T


def left_pair(table, place, own, other):
    order = other.shape[3]
    return pl.pallas_call(
        left_kernel,
        out_shape=jax.ShapeDtypeStruct((2, order, order), own.dtype),
        in_specs=[SMEM, SMEM, HBM, HBM],
        out_specs=VMEM,
        scratch_shapes=[
            pltpu.VMEM(other.shape, other.dtype),
            pltpu.VMEM(other.shape, other.dtype),
            pltpu.SemaphoreType.DMA((2,)),
        ],
        compiler_params=params(),
        name="left_pair",
    )(table, place, own, other)


def product_kernel(left, right, out):
    order = left.shape[2]
    b_re = right[:, 0].reshape(order, order)
    b_im = right[:, 1].reshape(order, order)
    step = order // BLOCKS
    for block in range(BLOCKS):
        rows = slice(block * step, (block + 1) * step)
        a_re = left[0, rows, :]
        a_im = left[1, rows, :]
        out[0, rows, :] = (dot(a_re, b_re) - dot(a_im, b_im)).astype(out.dtype)
        out[1, rows, :] = (dot(a_re, b_im) + dot(a_im, b_re)).astype(out.dtype)


def product(left, right):
    order = left.shape[2]
    return pl.pallas_call(
        product_kernel,
        out_shape=jax.ShapeDtypeStruct(left.shape, left.dtype),
        in_specs=[VMEM, VMEM],
        out_specs=VMEM,
        compiler_params=params(),
        name="product",
    )(left, right)


def panels_kernel(place, left_hbm, right_hbm, *refs):
    outs, (left, right, scratch, sems) = refs[:-4], refs[-4:]
    order = left.shape[2]
    width = right.shape[3]
    rows_each = right.shape[2]
    step = order // BLOCKS
    per = step // rows_each
    own = lax.rem(place[0], SET)
    copies = [pltpu.make_async_copy(right_hbm, right, sems.at[BLOCKS])]
    for block in range(BLOCKS):
        rows = slice(block * step, (block + 1) * step)
        copies.append(pltpu.make_async_copy(left_hbm.at[:, rows], left.at[:, rows], sems.at[block]))
    for copy in copies:
        copy.start()
    copies[0].wait()
    b_re = right[:, 0].reshape(order, width)
    b_im = right[:, 1].reshape(order, width)
    for block in range(BLOCKS):
        copies[block + 1].wait()
        rows = slice(block * step, (block + 1) * step)
        a_re = left[0, rows, :]
        a_im = left[1, rows, :]
        re = (dot(a_re, b_re) - dot(a_im, b_im)).astype(scratch.dtype)
        im = (dot(a_re, b_im) + dot(a_im, b_re)).astype(scratch.dtype)
        panels = slice(block * per, (block + 1) * per)
        scratch[panels, 0] = re.reshape(per, rows_each, width)
        scratch[panels, 1] = im.reshape(per, rows_each, width)
    for s, out in enumerate(outs):
        target = jnp.bitwise_xor(own, s)
        for owner in range(out.shape[0]):
            out[owner] = scratch[SET * owner + target]


def panels_of(place, left, right):
    count, two, rows, width = right.shape
    return pl.pallas_call(
        panels_kernel,
        out_shape=[jax.ShapeDtypeStruct((count // SET, two, rows, width), left.dtype)] * SET,
        in_specs=[SMEM, HBM, HBM],
        out_specs=[VMEM] * SET,
        scratch_shapes=[
            pltpu.VMEM(left.shape, left.dtype),
            pltpu.VMEM(right.shape, right.dtype),
            pltpu.VMEM(right.shape, right.dtype),
            pltpu.SemaphoreType.DMA((BLOCKS + 1,)),
        ],
        compiler_params=params(PANELS_VMEM_BYTES),
        name="panels",
    )(place, left, right)


def partial_kernel(table, place, *refs):
    pieces, outs, scratch = refs[:SET], refs[SET:-1], refs[-1]
    own = lax.rem(place[0], SET)
    mine = place[0] // SET
    for s, piece in enumerate(pieces):
        scratch[s] = piece[...]
    for slot in range(outs[0].shape[0]):
        one = jnp.bitwise_xor(table[6, slot], own)
        second = table[7, slot]
        two = jnp.bitwise_xor(jnp.maximum(second, 0), own)
        for e, out in enumerate(outs):
            owner = jnp.bitwise_xor(mine, e)
            other = scratch[two, owner].astype(jnp.float32)
            total = scratch[one, owner].astype(jnp.float32) + jnp.where(second >= 0, other, 0.0)
            out[slot] = total.astype(out.dtype)


def partial_sums(slots, table, place, pieces):
    sets = pieces[0].shape[0]
    shape = pieces[0].shape[1:]
    return pl.pallas_call(
        partial_kernel,
        out_shape=[jax.ShapeDtypeStruct((slots,) + shape, pieces[0].dtype)] * sets,
        in_specs=[SMEM, SMEM] + [VMEM] * SET,
        out_specs=[VMEM] * sets,
        scratch_shapes=[pltpu.VMEM((SET,) + pieces[0].shape, pieces[0].dtype)],
        compiler_params=params(),
        name="partial_sums",
    )(table, place, *pieces)


def diagrams_kernel(parts, sets, table, *refs):
    ins, out, held = refs[: parts * sets], refs[parts * sets], refs[parts * sets + 1]

    start = 0
    for j in range(parts):
        width = ins[j * sets].shape[3]
        for e in range(sets):
            held[e, :, :, :, start : start + width] = ins[j * sets + e][...]
        start += width

    for d in range(out.shape[0]):
        one, two = table[4, d], jnp.maximum(table[5, d], 0)
        first = held[one // SET, lax.rem(one, SET)].astype(jnp.float32)
        second = held[two // SET, lax.rem(two, SET)].astype(jnp.float32)
        out[d] = (first + jnp.where(table[5, d] >= 0, second, 0.0)).astype(out.dtype)


def diagrams_of(table, parts):
    slots, two, rows, _ = parts[0][0].shape
    sets = len(parts[0])
    diags = table.shape[1] // 2
    whole = sum(pieces[0].shape[3] for pieces in parts)
    dtype = parts[0][0].dtype
    return pl.pallas_call(
        functools.partial(diagrams_kernel, len(parts), sets),
        out_shape=jax.ShapeDtypeStruct((diags, two, rows, whole), dtype),
        in_specs=[SMEM] + [VMEM] * (sets * len(parts)),
        out_specs=VMEM,
        scratch_shapes=[pltpu.VMEM((sets, slots, two, rows, whole), dtype)],
        compiler_params=params(),
        name="diagrams",
    )(table, *[x for pieces in parts for x in pieces])


def exchange(x):
    return lax.all_to_all(x, "node", split_axis=0, concat_axis=0, tiled=True)


def after(x, earlier):
    return lax.optimization_barrier((x, earlier))[0]


def swap(x, size, shift):
    return lax.ppermute(x, "node", [(i, i ^ shift) for i in range(size)])


def tail(slots, size, table, place, picks, left, middle):
    left_middle = product(left, middle)
    done = middle
    parts = []
    for picked in picks:
        last = exchange(after(picked, done))
        if parts:
            last = after(last, parts[-1][0])
        sent = panels_of(place, left_middle, last)
        pieces = [sent[0]] + [swap(sent[s], size, s) for s in range(1, SET)]
        sums = partial_sums(slots, table, place, pieces)
        done = (last, left_middle)
        parts.append([sums[0]] + [swap(x, size, SET * e) for e, x in enumerate(sums) if e])
    return diagrams_of(table, parts)


def local(size, nodes, pair_nodes, prod_left, prod_right, prod_flag, prod_diag):
    place = lax.axis_index("node").astype(jnp.int32).reshape(1)
    order = nodes.shape[3]
    table = route(place, pair_nodes, prod_left, prod_right, prod_flag, prod_diag)
    own = exchange(pick(table, nodes, 0, 0, order))
    other = swap(own, size, 1)
    middle = exchange(after(pick(table, nodes, 1, 0, order), own))
    left = left_pair(table, place, own, other)
    widths = [order * share // sum(SHARES) for share in SHARES]
    picks = [pick(table, nodes, 2, sum(widths[:j]), width) for j, width in enumerate(widths)]
    few = functools.partial(tail, SET - 1, size)
    many = functools.partial(tail, SET, size)
    return lax.cond(table[8, 0] < SET, few, many, table, place, picks, left, middle)


def solution(mesh):
    placed = (P("grp", None, "node", None), P(), P(), P(), P(), P())
    return jax.shard_map(
        functools.partial(local, mesh.shape["node"]),
        mesh=mesh,
        in_specs=placed,
        out_specs=P("grp", None, "node", None),
        check_vma=False,
    )
```

```python
import functools

import jax
import jax.numpy as jnp
from jax import lax
from jax.experimental import pallas as pl
from jax.experimental.pallas import tpu as pltpu
from jax.sharding import PartitionSpec as P

SHARES = (1, 1)
SET = 4
BLOCKS = 4
VMEM_BYTES = 48 * 1024 * 1024
PANELS_VMEM_BYTES = 56 * 1024 * 1024
WHOLE_VMEM_BYTES = 60 * 1024 * 1024
SMEM = pl.BlockSpec(memory_space=pltpu.SMEM)
HBM = pl.BlockSpec(memory_space=pltpu.HBM)
VMEM = pl.BlockSpec(memory_space=pltpu.VMEM)


def params(limit=VMEM_BYTES):
    return pltpu.CompilerParams(vmem_limit_bytes=limit)


def route_kernel(
    prods, place_ref, pair_nodes, prod_left, prod_right, prod_flag, prod_diag, table, by_left, diag, mate, seen, kind, slots
):
    diags = prods // 2
    mine = place_ref[0] // SET

    def clear(k, carry):
        mate[k] = 0
        seen[k] = 0
        slots[k] = 0
        table[4, k] = -1
        table[5, k] = -1
        table[6, k] = 0
        table[7, k] = -1
        table[8, k] = 0
        return carry

    lax.fori_loop(0, prods, clear, 0)

    def rank(k, carry):
        own = prod_left[k]

        def count(j, total):
            other = prod_left[j]
            before = jnp.logical_or(other < own, jnp.logical_and(other == own, j < k))
            return total + before.astype(jnp.int32)

        at = lax.fori_loop(0, prods, count, 0, unroll=True)
        by_left[at] = k
        diag[at] = prod_diag[k]
        return carry

    lax.fori_loop(0, prods, rank, 0)

    def pair_up(s, carry):
        own = diag[s]

        def find(j, found):
            same = jnp.logical_and(diag[j] == own, j != s)
            return jnp.where(same, j, found)

        mate[s] = lax.fori_loop(0, prods, find, s, unroll=True)
        return carry

    lax.fori_loop(0, prods, pair_up, 0)

    def sibling_of(s):
        return s + 1 - 2 * lax.rem(s, 2)

    def kind_of(g, carry):
        def step(_, state):
            s, length = state
            back = s // 2 == g
            return jnp.where(back, s, mate[sibling_of(s)]), jnp.where(back, length, length + 1)

        _, length = lax.fori_loop(0, diags, step, (mate[2 * g + 1], 1))
        kind[g] = jnp.where(lax.rem(length, 2) == 0, 0, jnp.where(length == 1, 2, 1))
        return carry

    lax.fori_loop(0, diags, kind_of, 0)

    def add(device, s):
        k = by_left[s]
        right = prod_right[k]
        table[0, device] = pair_nodes[prod_left[k], lax.rem(device, 2)]
        table[1, device] = pair_nodes[right, 0]
        table[2, device] = pair_nodes[right, 1]
        table[3, device] = prod_flag[k]
        d = diag[s]
        owner = device // SET
        code = SET * owner
        earlier = table[4, d]
        shared = jnp.logical_and(earlier >= 0, earlier // SET == code // SET)
        slot = jnp.where(shared, earlier - code, slots[owner])

        @pl.when(jnp.logical_not(shared))
        def _():
            slots[owner] = slot + 1
            table[8, 0] = jnp.maximum(table[8, 0], slot + 1)
            table[jnp.where(earlier >= 0, 5, 4), d] = code + slot

        @pl.when(owner == mine)
        def _():
            table[jnp.where(shared, 7, 6), slot] = lax.rem(device, SET)

    def walk(n, carry):
        s, last = carry

        def first(j, found):
            g = diags - 1 - j
            own = kind[g]
            worth = jnp.where(own == 0, 3, jnp.where(own == last, 1, 2))
            worth = jnp.where(seen[g] == 0, worth, 0)
            best, at = found
            return jnp.maximum(best, worth), jnp.where(worth >= best, g, at)

        _, fresh = lax.fori_loop(0, diags, first, (1, 0), unroll=True)
        s = jnp.where(seen[s // 2] == 0, s, 2 * fresh)
        seen[s // 2] = 1
        add(2 * n, s)
        add(2 * n + 1, sibling_of(s))
        return mate[sibling_of(s)], kind[s // 2]

    lax.fori_loop(0, diags, walk, (0, 2))


def route(place, pair_nodes, prod_left, prod_right, prod_flag, prod_diag):
    prods = prod_left.shape[0]
    return pl.pallas_call(
        functools.partial(route_kernel, prods),
        out_shape=jax.ShapeDtypeStruct((9, prods), jnp.int32),
        in_specs=[SMEM] * 6,
        out_specs=SMEM,
        scratch_shapes=[pltpu.SMEM((prods,), jnp.int32)] * 6,
        name="route",
    )(place, pair_nodes, prod_left, prod_right, prod_flag, prod_diag)


def pick_kernel(row, start, table, nodes, out, held, reads, writes):
    count, _, _, width = out.shape

    def read(t):
        node = nodes.at[table[row, t], :, :, pl.ds(start, width)]
        return pltpu.make_async_copy(node, held.at[t], reads.at[t])

    def write(t):
        return pltpu.make_async_copy(held.at[t], out.at[t], writes.at[t])

    for t in range(count):
        read(t).start()
    for t in range(count):
        read(t).wait()
        write(t).start()
    for t in range(count):
        write(t).wait()


def pick(table, nodes, row, start, width):
    count = table.shape[1]
    shape = (count, nodes.shape[1], nodes.shape[2], width)
    return pl.pallas_call(
        functools.partial(pick_kernel, row, start),
        out_shape=jax.ShapeDtypeStruct(shape, nodes.dtype),
        in_specs=[SMEM, HBM],
        out_specs=HBM,
        scratch_shapes=[
            pltpu.VMEM(shape, nodes.dtype),
            pltpu.SemaphoreType.DMA((count,)),
            pltpu.SemaphoreType.DMA((count,)),
        ],
        compiler_params=params(WHOLE_VMEM_BYTES),
        name="pick",
    )(table, nodes)


def pick_sets_kernel(row, place, table, nodes, *refs):
    outs, (held, reads, writes) = refs[:SET], refs[SET:]
    sets = outs[0].shape[0]
    own = lax.rem(place[0], SET)
    which = [(s, q) for s in range(SET) for q in range(sets)]

    def read(s, q):
        node = nodes.at[table[row, SET * q + jnp.bitwise_xor(own, s)]]
        return pltpu.make_async_copy(node, held.at[s, q], reads.at[s, q])

    def write(s, q):
        return pltpu.make_async_copy(held.at[s, q], outs[s].at[q], writes.at[s, q])

    for s, q in which:
        read(s, q).start()
    for s, q in which:
        read(s, q).wait()
        write(s, q).start()
    for s, q in which:
        write(s, q).wait()


def pick_sets(table, place, nodes, row):
    sets = table.shape[1] // SET
    shape = nodes.shape[1:]
    return pl.pallas_call(
        functools.partial(pick_sets_kernel, row),
        out_shape=[jax.ShapeDtypeStruct((sets,) + shape, nodes.dtype)] * SET,
        in_specs=[SMEM, SMEM, HBM],
        out_specs=[HBM] * SET,
        scratch_shapes=[
            pltpu.VMEM((SET, sets) + shape, nodes.dtype),
            pltpu.SemaphoreType.DMA((SET, sets)),
            pltpu.SemaphoreType.DMA((SET, sets)),
        ],
        compiler_params=params(WHOLE_VMEM_BYTES),
        name="pick_sets",
    )(place, table, nodes)


def regroup_kernel(starts, *refs):
    pieces, outs, (held, reads, writes) = refs[:SET], refs[SET:-3], refs[-3:]
    sets = pieces[0].shape[0]
    which = [(s, q) for q in range(sets) for s in range(SET)]

    def read(s, q):
        return pltpu.make_async_copy(pieces[s].at[q], held.at[s, q], reads.at[s, q])

    def write(s, q, j):
        columns = held.at[s, q, :, :, pl.ds(starts[j], outs[j].shape[4])]
        return pltpu.make_async_copy(columns, outs[j].at[q, s], writes.at[s, q, j])

    for s, q in which:
        read(s, q).start()
    for s, q in which:
        read(s, q).wait()
        for j in range(len(starts)):
            write(s, q, j).start()
    for s, q in which:
        for j in range(len(starts)):
            write(s, q, j).wait()


def regroup(pieces, widths):
    sets, two, rows, _ = pieces[0].shape
    dtype = pieces[0].dtype
    starts = [sum(widths[:j]) for j in range(len(widths))]
    return pl.pallas_call(
        functools.partial(regroup_kernel, starts),
        out_shape=[jax.ShapeDtypeStruct((sets, SET, two, rows, w), dtype) for w in widths],
        in_specs=[HBM] * SET,
        out_specs=[HBM] * len(widths),
        scratch_shapes=[
            pltpu.VMEM((SET,) + pieces[0].shape, dtype),
            pltpu.SemaphoreType.DMA((SET, sets)),
            pltpu.SemaphoreType.DMA((SET, sets, len(widths))),
        ],
        compiler_params=params(WHOLE_VMEM_BYTES),
        name="regroup",
    )(*pieces)


def dot(a, b):
    return jnp.dot(a, b, preferred_element_type=jnp.float32)


def left_kernel(table, place, own, other, out, left, right, sems):
    order = left.shape[2] * left.shape[0]
    core = lax.rem(place[0], 2)
    flag = table[3, place[0]]

    def load(first, second):
        one = pltpu.make_async_copy(first, left, sems.at[0])
        two = pltpu.make_async_copy(second, right, sems.at[1])
        one.start()
        two.start()
        one.wait()
        two.wait()

    @pl.when(core == 0)
    def _():
        load(own, other)

    @pl.when(core == 1)
    def _():
        load(other, own)

    b_re = right[:, 0].reshape(order, order)
    b_im = right[:, 1].reshape(order, order)
    step = order // 4
    per = left.shape[0] // 4
    for block in range(4):
        a_re = left[block * per : (block + 1) * per, 0].reshape(step, order)
        a_im = left[block * per : (block + 1) * per, 1].reshape(step, order)
        re = (dot(a_re, b_re) - dot(a_im, b_im)).astype(out.dtype)
        im = (dot(a_re, b_im) + dot(a_im, b_re)).astype(out.dtype)

        @pl.when(flag == 0)
        def _():
            out[0, block * step : (block + 1) * step, :] = re
            out[1, block * step : (block + 1) * step, :] = im

        @pl.when(flag == 1)
        def _():
            out[0, :, block * step : (block + 1) * step] = re.T
            out[1, :, block * step : (block + 1) * step] = -im.T


def left_pair(table, place, own, other):
    order = other.shape[3]
    return pl.pallas_call(
        left_kernel,
        out_shape=jax.ShapeDtypeStruct((2, order, order), own.dtype),
        in_specs=[SMEM, SMEM, HBM, HBM],
        out_specs=VMEM,
        scratch_shapes=[
            pltpu.VMEM(other.shape, other.dtype),
            pltpu.VMEM(other.shape, other.dtype),
            pltpu.SemaphoreType.DMA((2,)),
        ],
        compiler_params=params(),
        name="left_pair",
    )(table, place, own, other)


def product_kernel(left, right, out):
    order = left.shape[2]
    b_re = right[:, 0].reshape(order, order)
    b_im = right[:, 1].reshape(order, order)
    step = order // BLOCKS
    for block in range(BLOCKS):
        rows = slice(block * step, (block + 1) * step)
        a_re = left[0, rows, :]
        a_im = left[1, rows, :]
        out[0, rows, :] = (dot(a_re, b_re) - dot(a_im, b_im)).astype(out.dtype)
        out[1, rows, :] = (dot(a_re, b_im) + dot(a_im, b_re)).astype(out.dtype)


def product(left, right):
    order = left.shape[2]
    return pl.pallas_call(
        product_kernel,
        out_shape=jax.ShapeDtypeStruct(left.shape, left.dtype),
        in_specs=[VMEM, VMEM],
        out_specs=VMEM,
        compiler_params=params(),
        name="product",
    )(left, right)


def panels_kernel(place, left_hbm, right_hbm, *refs):
    outs, (left, right, scratch, sems, right_sems) = refs[:-5], refs[-5:]
    order = left.shape[2]
    width = right.shape[3]
    rows_each = right.shape[2]
    step = order // BLOCKS
    per = step // rows_each
    own = lax.rem(place[0], SET)
    rights, lefts = [], []
    for q in range(right_hbm.shape[0]):
        for s in range(SET):
            device = SET * q + jnp.bitwise_xor(own, s)
            sem = right_sems.at[q, s]
            rights.append(pltpu.make_async_copy(right_hbm.at[q, s], right.at[device], sem))
    for block in range(BLOCKS):
        rows = slice(block * step, (block + 1) * step)
        lefts.append(pltpu.make_async_copy(left_hbm.at[:, rows], left.at[:, rows], sems.at[block]))
    for copy in rights + lefts:
        copy.start()
    for copy in rights:
        copy.wait()
    b_re = right[:, 0].reshape(order, width)
    b_im = right[:, 1].reshape(order, width)
    for block in range(BLOCKS):
        lefts[block].wait()
        rows = slice(block * step, (block + 1) * step)
        a_re = left[0, rows, :]
        a_im = left[1, rows, :]
        re = (dot(a_re, b_re) - dot(a_im, b_im)).astype(scratch.dtype)
        im = (dot(a_re, b_im) + dot(a_im, b_re)).astype(scratch.dtype)
        panels = slice(block * per, (block + 1) * per)
        scratch[panels, 0] = re.reshape(per, rows_each, width)
        scratch[panels, 1] = im.reshape(per, rows_each, width)
    for s, out in enumerate(outs):
        target = jnp.bitwise_xor(own, s)
        for owner in range(out.shape[0]):
            out[owner] = scratch[SET * owner + target]


def panels_of(place, left, right):
    sets, _, two, rows, width = right.shape
    whole = pltpu.VMEM((sets * SET, two, rows, width), right.dtype)
    return pl.pallas_call(
        panels_kernel,
        out_shape=[jax.ShapeDtypeStruct((sets, two, rows, width), left.dtype)] * SET,
        in_specs=[SMEM, HBM, HBM],
        out_specs=[VMEM] * SET,
        scratch_shapes=[
            pltpu.VMEM(left.shape, left.dtype),
            whole,
            whole,
            pltpu.SemaphoreType.DMA((BLOCKS,)),
            pltpu.SemaphoreType.DMA((sets, SET)),
        ],
        compiler_params=params(PANELS_VMEM_BYTES),
        name="panels",
    )(place, left, right)


def sums_kernel(whole, table, place, *refs):
    pieces, outs, rest, scratch = refs[:SET], refs[SET:-2], refs[-2], refs[-1]
    own = lax.rem(place[0], SET)
    mine = place[0] // SET
    for s, piece in enumerate(pieces):
        scratch[s] = piece[...]

    def sum_at(slot, owner):
        one = jnp.bitwise_xor(table[6, slot], own)
        second = table[7, slot]
        two = jnp.bitwise_xor(jnp.maximum(second, 0), own)
        other = scratch[two, owner].astype(jnp.float32)
        total = scratch[one, owner].astype(jnp.float32) + jnp.where(second >= 0, other, 0.0)
        return total.astype(rest.dtype)

    for slot in range(SET - 1):
        for e in range(rest.shape[0]):
            if whole:
                outs[0][e, slot] = sum_at(slot, e)
            else:
                outs[e][slot] = sum_at(slot, jnp.bitwise_xor(mine, e))

    @pl.when(table[8, 0] == SET)
    def _():
        for e in range(rest.shape[0]):
            rest[e, 0] = sum_at(SET - 1, e)


def sums_of(table, place, pieces, whole):
    sets = pieces[0].shape[0]
    shape = pieces[0].shape[1:]
    dtype = pieces[0].dtype
    outs = [jax.ShapeDtypeStruct((sets, SET - 1) + shape, dtype)]
    if not whole:
        outs = [jax.ShapeDtypeStruct((SET - 1,) + shape, dtype)] * sets
    outs.append(jax.ShapeDtypeStruct((sets, 1) + shape, dtype))
    *sums, rest = pl.pallas_call(
        functools.partial(sums_kernel, whole),
        out_shape=outs,
        in_specs=[SMEM, SMEM] + [VMEM] * SET,
        out_specs=[VMEM] * len(outs),
        scratch_shapes=[pltpu.VMEM((SET,) + pieces[0].shape, dtype)],
        compiler_params=params(),
        name="sums",
    )(table, place, *pieces)
    return sums, rest


def diagrams_kernel(whole_parts, table, place, *refs):
    wholes, rests = refs[:whole_parts], refs[whole_parts : 2 * whole_parts + 1]
    pieces, (out, held) = refs[2 * whole_parts + 1 : -2], refs[-2:]
    mine = place[0] // SET
    for e, piece in enumerate(pieces):
        held[jnp.bitwise_xor(mine, e)] = piece[...]

    def write(wide):
        start = 0
        for part, rest in zip([*wholes, held], rests):
            width = part.shape[4]

            def sum_at(code):
                owner, slot = code // SET, lax.rem(code, SET)
                if not wide:
                    return part[owner, slot].astype(jnp.float32)
                usual = part[owner, jnp.minimum(slot, SET - 2)].astype(jnp.float32)
                return jnp.where(slot == SET - 1, rest[owner, 0].astype(jnp.float32), usual)

            for d in range(out.shape[0]):
                second = sum_at(jnp.maximum(table[5, d], 0))
                total = sum_at(table[4, d]) + jnp.where(table[5, d] >= 0, second, 0.0)
                out[d, :, :, start : start + width] = total.astype(out.dtype)
            start += width

    @pl.when(table[8, 0] < SET)
    def _():
        write(False)

    @pl.when(table[8, 0] == SET)
    def _():
        write(True)


def diagrams_of(table, place, wholes, rests, pieces):
    slots, two, rows, width = pieces[0].shape
    order = width + sum(part.shape[4] for part in wholes)
    dtype = pieces[0].dtype
    operands = [*wholes, *rests, *pieces]
    return pl.pallas_call(
        functools.partial(diagrams_kernel, len(wholes)),
        out_shape=jax.ShapeDtypeStruct((table.shape[1] // 2, two, rows, order), dtype),
        in_specs=[SMEM, SMEM] + [VMEM] * len(operands),
        out_specs=VMEM,
        scratch_shapes=[pltpu.VMEM((len(pieces),) + pieces[0].shape, dtype)],
        compiler_params=params(),
        name="diagrams",
    )(table, place, *operands)


def exchange(x, groups=None):
    return lax.all_to_all(
        x, "node", split_axis=0, concat_axis=0, axis_index_groups=groups, tiled=True
    )


def after(x, earlier):
    return lax.optimization_barrier((x, earlier))[0]


def swap(x, size, shift):
    return lax.ppermute(x, "node", [(i, i ^ shift) for i in range(size)])


def within(pieces, size):
    return [pieces[0]] + [swap(pieces[s], size, s) for s in range(1, SET)]


def local(size, nodes, pair_nodes, prod_left, prod_right, prod_flag, prod_diag):
    place = lax.axis_index("node").astype(jnp.int32).reshape(1)
    order = nodes.shape[3]
    widths = [order * share // sum(SHARES) for share in SHARES]
    across = [list(range(i, size, SET)) for i in range(SET)]
    table = route(place, pair_nodes, prod_left, prod_right, prod_flag, prod_diag)
    own = exchange(pick(table, nodes, 0, 0, order))
    pieces = within(pick_sets(table, place, nodes, 2), size)
    other = swap(own, size, 1)
    middle = exchange(after(pick(table, nodes, 1, 0, order), (own, pieces[2])))
    left = left_pair(table, place, own, other)
    sents = regroup(pieces, widths)
    left_middle = product(left, middle)
    done, wholes, rests = (middle, left), [], []
    for j, sent in enumerate(sents):
        last = exchange(after(sent, done), across)
        done = (last, left_middle)
        if wholes:
            last = after(last, sums)
        panels = within(panels_of(place, left_middle, last), size)
        if wholes:
            panels = after(panels, wholes[-1])
        sums, rest = sums_of(table, place, panels, j < len(sents) - 1)
        rests.append(rest)
        if j < len(sents) - 1:
            wholes.append(exchange(sums[0], across))
    sums = [x if e == 0 else swap(x, size, SET * e) for e, x in enumerate(sums)]

    def move(rests):
        return [exchange(rest, across) for rest in rests]

    rests = lax.cond(table[8, 0] < SET, lambda rests: rests, move, rests)
    return diagrams_of(table, place, wholes, rests, sums)


def solution(mesh):
    placed = (P("grp", None, "node", None), P(), P(), P(), P(), P())
    return jax.shard_map(
        functools.partial(local, mesh.shape["node"]),
        mesh=mesh,
        in_specs=placed,
        out_specs=P("grp", None, "node", None),
        check_vma=False,
    )
```

```python
import functools

import jax
import jax.numpy as jnp
from jax import lax
from jax.experimental import pallas as pl
from jax.experimental.pallas import tpu as pltpu
from jax.sharding import PartitionSpec as P

SHARES = (1, 1)
SET = 4
BLOCKS = 2
VMEM_BYTES = 48 * 1024 * 1024
PANELS_VMEM_BYTES = 62 * 1024 * 1024
WHOLE_VMEM_BYTES = 60 * 1024 * 1024
SMEM = pl.BlockSpec(memory_space=pltpu.SMEM)
HBM = pl.BlockSpec(memory_space=pltpu.HBM)
VMEM = pl.BlockSpec(memory_space=pltpu.VMEM)


def params(limit=VMEM_BYTES):
    return pltpu.CompilerParams(vmem_limit_bytes=limit)


def route_kernel(
    prods, place_ref, pair_nodes, prod_left, prod_right, prod_flag, prod_diag, table, by_left, diag, mate, seen, kind, slots
):
    diags = prods // 2
    mine = place_ref[0] // SET

    def clear(k, carry):
        mate[k] = 0
        seen[k] = 0
        slots[k] = 0
        table[4, k] = -1
        table[5, k] = -1
        table[6, k] = 0
        table[7, k] = -1
        table[8, k] = 0
        return carry

    lax.fori_loop(0, prods, clear, 0)

    def rank(k, carry):
        own = prod_left[k]

        def count(j, total):
            other = prod_left[j]
            before = jnp.logical_or(other < own, jnp.logical_and(other == own, j < k))
            return total + before.astype(jnp.int32)

        at = lax.fori_loop(0, prods, count, 0, unroll=True)
        by_left[at] = k
        diag[at] = prod_diag[k]
        return carry

    lax.fori_loop(0, prods, rank, 0)

    def pair_up(s, carry):
        own = diag[s]

        def find(j, found):
            same = jnp.logical_and(diag[j] == own, j != s)
            return jnp.where(same, j, found)

        mate[s] = lax.fori_loop(0, prods, find, s, unroll=True)
        return carry

    lax.fori_loop(0, prods, pair_up, 0)

    def sibling_of(s):
        return s + 1 - 2 * lax.rem(s, 2)

    def kind_of(g, carry):
        def step(_, state):
            s, length = state
            back = s // 2 == g
            return jnp.where(back, s, mate[sibling_of(s)]), jnp.where(back, length, length + 1)

        _, length = lax.fori_loop(0, diags, step, (mate[2 * g + 1], 1))
        kind[g] = jnp.where(lax.rem(length, 2) == 0, 0, jnp.where(length == 1, 2, 1))
        return carry

    lax.fori_loop(0, diags, kind_of, 0)

    def add(device, s):
        k = by_left[s]
        right = prod_right[k]
        table[0, device] = pair_nodes[prod_left[k], lax.rem(device, 2)]
        table[1, device] = pair_nodes[right, 0]
        table[2, device] = pair_nodes[right, 1]
        table[3, device] = prod_flag[k]
        d = diag[s]
        owner = device // SET
        code = SET * owner
        earlier = table[4, d]
        shared = jnp.logical_and(earlier >= 0, earlier // SET == code // SET)
        slot = jnp.where(shared, earlier - code, slots[owner])

        @pl.when(jnp.logical_not(shared))
        def _():
            slots[owner] = slot + 1
            table[8, 0] = jnp.maximum(table[8, 0], slot + 1)
            table[jnp.where(earlier >= 0, 5, 4), d] = code + slot

        @pl.when(owner == mine)
        def _():
            table[jnp.where(shared, 7, 6), slot] = lax.rem(device, SET)

    def walk(n, carry):
        s, last = carry

        def first(j, found):
            g = diags - 1 - j
            own = kind[g]
            worth = jnp.where(own == 0, 3, jnp.where(own == last, 1, 2))
            worth = jnp.where(seen[g] == 0, worth, 0)
            best, at = found
            return jnp.maximum(best, worth), jnp.where(worth >= best, g, at)

        _, fresh = lax.fori_loop(0, diags, first, (1, 0), unroll=True)
        s = jnp.where(seen[s // 2] == 0, s, 2 * fresh)
        seen[s // 2] = 1
        add(2 * n, s)
        add(2 * n + 1, sibling_of(s))
        return mate[sibling_of(s)], kind[s // 2]

    lax.fori_loop(0, diags, walk, (0, 2))


def route(place, pair_nodes, prod_left, prod_right, prod_flag, prod_diag):
    prods = prod_left.shape[0]
    return pl.pallas_call(
        functools.partial(route_kernel, prods),
        out_shape=jax.ShapeDtypeStruct((9, prods), jnp.int32),
        in_specs=[SMEM] * 6,
        out_specs=SMEM,
        scratch_shapes=[pltpu.SMEM((prods,), jnp.int32)] * 6,
        name="route",
    )(place, pair_nodes, prod_left, prod_right, prod_flag, prod_diag)


def pick_kernel(row, start, table, nodes, out, held, reads, writes):
    count, _, _, width = out.shape

    def read(t):
        node = nodes.at[table[row, t], :, :, pl.ds(start, width)]
        return pltpu.make_async_copy(node, held.at[t], reads.at[t])

    def write(t):
        return pltpu.make_async_copy(held.at[t], out.at[t], writes.at[t])

    for t in range(count):
        read(t).start()
    for t in range(count):
        read(t).wait()
        write(t).start()
    for t in range(count):
        write(t).wait()


def pick(table, nodes, row, start, width):
    count = table.shape[1]
    shape = (count, nodes.shape[1], nodes.shape[2], width)
    return pl.pallas_call(
        functools.partial(pick_kernel, row, start),
        out_shape=jax.ShapeDtypeStruct(shape, nodes.dtype),
        in_specs=[SMEM, HBM],
        out_specs=HBM,
        scratch_shapes=[
            pltpu.VMEM(shape, nodes.dtype),
            pltpu.SemaphoreType.DMA((count,)),
            pltpu.SemaphoreType.DMA((count,)),
        ],
        compiler_params=params(WHOLE_VMEM_BYTES),
        name="pick",
    )(table, nodes)


def pick_sets_kernel(row, place, table, nodes, *refs):
    outs, (held, reads, writes) = refs[:SET], refs[SET:]
    sets = outs[0].shape[0]
    own = lax.rem(place[0], SET)
    which = [(s, q) for s in range(SET) for q in range(sets)]

    def read(s, q):
        node = nodes.at[table[row, SET * q + jnp.bitwise_xor(own, s)]]
        return pltpu.make_async_copy(node, held.at[s, q], reads.at[s, q])

    def write(s, q):
        return pltpu.make_async_copy(held.at[s, q], outs[s].at[q], writes.at[s, q])

    for s, q in which:
        read(s, q).start()
    for s, q in which:
        read(s, q).wait()
        write(s, q).start()
    for s, q in which:
        write(s, q).wait()


def pick_sets(table, place, nodes, row):
    sets = table.shape[1] // SET
    shape = nodes.shape[1:]
    return pl.pallas_call(
        functools.partial(pick_sets_kernel, row),
        out_shape=[jax.ShapeDtypeStruct((sets,) + shape, nodes.dtype)] * SET,
        in_specs=[SMEM, SMEM, HBM],
        out_specs=[HBM] * SET,
        scratch_shapes=[
            pltpu.VMEM((SET, sets) + shape, nodes.dtype),
            pltpu.SemaphoreType.DMA((SET, sets)),
            pltpu.SemaphoreType.DMA((SET, sets)),
        ],
        compiler_params=params(WHOLE_VMEM_BYTES),
        name="pick_sets",
    )(place, table, nodes)


def regroup_kernel(starts, *refs):
    pieces, outs, (held, reads, writes) = refs[:SET], refs[SET:-3], refs[-3:]
    sets = pieces[0].shape[0]
    which = [(s, q) for q in range(sets) for s in range(SET)]

    def read(s, q):
        return pltpu.make_async_copy(pieces[s].at[q], held.at[s, q], reads.at[s, q])

    def write(s, q, j):
        columns = held.at[s, q, :, :, pl.ds(starts[j], outs[j].shape[4])]
        return pltpu.make_async_copy(columns, outs[j].at[q, s], writes.at[s, q, j])

    for s, q in which:
        read(s, q).start()
    for s, q in which:
        read(s, q).wait()
        for j in range(len(starts)):
            write(s, q, j).start()
    for s, q in which:
        for j in range(len(starts)):
            write(s, q, j).wait()


def regroup(pieces, widths):
    sets, two, rows, _ = pieces[0].shape
    dtype = pieces[0].dtype
    starts = [sum(widths[:j]) for j in range(len(widths))]
    return pl.pallas_call(
        functools.partial(regroup_kernel, starts),
        out_shape=[jax.ShapeDtypeStruct((sets, SET, two, rows, w), dtype) for w in widths],
        in_specs=[HBM] * SET,
        out_specs=[HBM] * len(widths),
        scratch_shapes=[
            pltpu.VMEM((SET,) + pieces[0].shape, dtype),
            pltpu.SemaphoreType.DMA((SET, sets)),
            pltpu.SemaphoreType.DMA((SET, sets, len(widths))),
        ],
        compiler_params=params(WHOLE_VMEM_BYTES),
        name="regroup",
    )(*pieces)


def dot(a, b):
    return jnp.dot(a, b, preferred_element_type=jnp.float32)


def left_kernel(table, place, own, other, out, left, right, sems):
    order = left.shape[2] * left.shape[0]
    core = lax.rem(place[0], 2)
    flag = table[3, place[0]]

    def load(first, second):
        one = pltpu.make_async_copy(first, left, sems.at[0])
        two = pltpu.make_async_copy(second, right, sems.at[1])
        one.start()
        two.start()
        one.wait()
        two.wait()

    @pl.when(core == 0)
    def _():
        load(own, other)

    @pl.when(core == 1)
    def _():
        load(other, own)

    b_re = right[:, 0].reshape(order, order)
    b_im = right[:, 1].reshape(order, order)
    step = order // 4
    per = left.shape[0] // 4
    for block in range(4):
        a_re = left[block * per : (block + 1) * per, 0].reshape(step, order)
        a_im = left[block * per : (block + 1) * per, 1].reshape(step, order)
        re = (dot(a_re, b_re) - dot(a_im, b_im)).astype(out.dtype)
        im = (dot(a_re, b_im) + dot(a_im, b_re)).astype(out.dtype)

        @pl.when(flag == 0)
        def _():
            out[0, block * step : (block + 1) * step, :] = re
            out[1, block * step : (block + 1) * step, :] = im

        @pl.when(flag == 1)
        def _():
            out[0, :, block * step : (block + 1) * step] = re.T
            out[1, :, block * step : (block + 1) * step] = -im.T


def left_pair(table, place, own, other):
    order = other.shape[3]
    return pl.pallas_call(
        left_kernel,
        out_shape=jax.ShapeDtypeStruct((2, order, order), own.dtype),
        in_specs=[SMEM, SMEM, HBM, HBM],
        out_specs=VMEM,
        scratch_shapes=[
            pltpu.VMEM(other.shape, other.dtype),
            pltpu.VMEM(other.shape, other.dtype),
            pltpu.SemaphoreType.DMA((2,)),
        ],
        compiler_params=params(PANELS_VMEM_BYTES),
        name="left_pair",
    )(table, place, own, other)


def product_kernel(left, right, out):
    order = left.shape[2]
    b_re = right[:, 0].reshape(order, order)
    b_im = right[:, 1].reshape(order, order)
    step = order // BLOCKS
    for block in range(BLOCKS):
        rows = slice(block * step, (block + 1) * step)
        a_re = left[0, rows, :]
        a_im = left[1, rows, :]
        out[0, rows, :] = (dot(a_re, b_re) - dot(a_im, b_im)).astype(out.dtype)
        out[1, rows, :] = (dot(a_re, b_im) + dot(a_im, b_re)).astype(out.dtype)


def product(left, right):
    order = left.shape[2]
    return pl.pallas_call(
        product_kernel,
        out_shape=jax.ShapeDtypeStruct(left.shape, left.dtype),
        in_specs=[VMEM, VMEM],
        out_specs=VMEM,
        compiler_params=params(PANELS_VMEM_BYTES),
        name="product",
    )(left, right)


def panels_kernel(place, left_hbm, right_hbm, *refs):
    outs, (left, right, scratch, sems, right_sems) = refs[:-5], refs[-5:]
    order = left.shape[2]
    width = right.shape[3]
    rows_each = right.shape[2]
    step = order // BLOCKS
    per = step // rows_each
    own = lax.rem(place[0], SET)
    rights, lefts = [], []
    for q in range(right_hbm.shape[0]):
        for s in range(SET):
            device = SET * q + jnp.bitwise_xor(own, s)
            sem = right_sems.at[q, s]
            rights.append(pltpu.make_async_copy(right_hbm.at[q, s], right.at[device], sem))
    for block in range(BLOCKS):
        rows = slice(block * step, (block + 1) * step)
        lefts.append(pltpu.make_async_copy(left_hbm.at[:, rows], left.at[:, rows], sems.at[block]))
    for copy in rights + lefts:
        copy.start()
    for copy in rights:
        copy.wait()
    b_re = right[:, 0].reshape(order, width)
    b_im = right[:, 1].reshape(order, width)
    for block in range(BLOCKS):
        lefts[block].wait()
        rows = slice(block * step, (block + 1) * step)
        a_re = left[0, rows, :]
        a_im = left[1, rows, :]
        re = (dot(a_re, b_re) - dot(a_im, b_im)).astype(scratch.dtype)
        im = (dot(a_re, b_im) + dot(a_im, b_re)).astype(scratch.dtype)
        panels = slice(block * per, (block + 1) * per)
        scratch[panels, 0] = re.reshape(per, rows_each, width)
        scratch[panels, 1] = im.reshape(per, rows_each, width)
    for s, out in enumerate(outs):
        target = jnp.bitwise_xor(own, s)
        for owner in range(out.shape[0]):
            out[owner] = scratch[SET * owner + target]


def panels_of(place, left, right):
    sets, _, two, rows, width = right.shape
    whole = pltpu.VMEM((sets * SET, two, rows, width), right.dtype)
    return pl.pallas_call(
        panels_kernel,
        out_shape=[jax.ShapeDtypeStruct((sets, two, rows, width), left.dtype)] * SET,
        in_specs=[SMEM, HBM, HBM],
        out_specs=[VMEM] * SET,
        scratch_shapes=[
            pltpu.VMEM(left.shape, left.dtype),
            whole,
            whole,
            pltpu.SemaphoreType.DMA((BLOCKS,)),
            pltpu.SemaphoreType.DMA((sets, SET)),
        ],
        compiler_params=params(PANELS_VMEM_BYTES),
        name="panels",
    )(place, left, right)


def sums_kernel(whole, table, place, *refs):
    pieces, outs, rest, scratch = refs[:SET], refs[SET:-2], refs[-2], refs[-1]
    own = lax.rem(place[0], SET)
    mine = place[0] // SET
    for s, piece in enumerate(pieces):
        scratch[s] = piece[...]

    def sum_at(slot, owner):
        one = jnp.bitwise_xor(table[6, slot], own)
        second = table[7, slot]
        two = jnp.bitwise_xor(jnp.maximum(second, 0), own)
        other = scratch[two, owner].astype(jnp.float32)
        total = scratch[one, owner].astype(jnp.float32) + jnp.where(second >= 0, other, 0.0)
        return total.astype(rest.dtype)

    for slot in range(SET - 1):
        for e in range(rest.shape[0]):
            if whole:
                outs[0][e, slot] = sum_at(slot, e)
            else:
                outs[e][slot] = sum_at(slot, jnp.bitwise_xor(mine, e))

    @pl.when(table[8, 0] == SET)
    def _():
        for e in range(rest.shape[0]):
            rest[e, 0] = sum_at(SET - 1, e)


def sums_of(table, place, pieces, whole):
    sets = pieces[0].shape[0]
    shape = pieces[0].shape[1:]
    dtype = pieces[0].dtype
    outs = [jax.ShapeDtypeStruct((sets, SET - 1) + shape, dtype)]
    if not whole:
        outs = [jax.ShapeDtypeStruct((SET - 1,) + shape, dtype)] * sets
    outs.append(jax.ShapeDtypeStruct((sets, 1) + shape, dtype))
    *sums, rest = pl.pallas_call(
        functools.partial(sums_kernel, whole),
        out_shape=outs,
        in_specs=[SMEM, SMEM] + [VMEM] * SET,
        out_specs=[VMEM] * len(outs),
        scratch_shapes=[pltpu.VMEM((SET,) + pieces[0].shape, dtype)],
        compiler_params=params(),
        name="sums",
    )(table, place, *pieces)
    return sums, rest


def diagrams_kernel(whole_parts, table, place, *refs):
    wholes, rests = refs[:whole_parts], refs[whole_parts : 2 * whole_parts + 1]
    pieces, (out, held, lasts, sems) = refs[2 * whole_parts + 1 : -4], refs[-4:]
    mine = place[0] // SET
    for e, piece in enumerate(pieces):
        held[jnp.bitwise_xor(mine, e)] = piece[...]

    def write(wide):
        start = 0
        for part in [*wholes, held]:
            width = part.shape[4]
            columns = slice(start, start + width)

            def sum_at(code):
                owner, slot = code // SET, lax.rem(code, SET)
                if not wide:
                    return part[owner, slot].astype(jnp.float32)
                usual = part[owner, jnp.minimum(slot, SET - 2)].astype(jnp.float32)
                last = lasts[owner, 0, :, :, columns].astype(jnp.float32)
                return jnp.where(slot == SET - 1, last, usual)

            for d in range(out.shape[0]):
                second = sum_at(jnp.maximum(table[5, d], 0))
                total = sum_at(table[4, d]) + jnp.where(table[5, d] >= 0, second, 0.0)
                out[d, :, :, columns] = total.astype(out.dtype)
            start += width

    @pl.when(table[8, 0] < SET)
    def _():
        write(False)

    @pl.when(table[8, 0] == SET)
    def _():
        start, copies = 0, []
        for j, rest in enumerate(rests):
            columns = pl.ds(start, rest.shape[4])
            start += rest.shape[4]
            copies.append(
                pltpu.make_async_copy(rest, lasts.at[:, :, :, :, columns], sems.at[j])
            )
        for copy in copies:
            copy.start()
        for copy in copies:
            copy.wait()
        write(True)


def diagrams_of(table, place, wholes, rests, pieces):
    slots, two, rows, width = pieces[0].shape
    order = width + sum(part.shape[4] for part in wholes)
    dtype = pieces[0].dtype
    operands = [*wholes, *rests, *pieces]
    return pl.pallas_call(
        functools.partial(diagrams_kernel, len(wholes)),
        out_shape=jax.ShapeDtypeStruct((table.shape[1] // 2, two, rows, order), dtype),
        in_specs=[SMEM, SMEM] + [VMEM] * len(wholes) + [HBM] * len(rests) + [VMEM] * len(pieces),
        out_specs=VMEM,
        scratch_shapes=[
            pltpu.VMEM((len(pieces),) + pieces[0].shape, dtype),
            pltpu.VMEM((len(pieces), 1, two, rows, order), dtype),
            pltpu.SemaphoreType.DMA((len(rests),)),
        ],
        compiler_params=params(),
        name="diagrams",
    )(table, place, *operands)


def exchange(x, groups=None):
    return lax.all_to_all(
        x, "node", split_axis=0, concat_axis=0, axis_index_groups=groups, tiled=True
    )


def after(x, earlier):
    return lax.optimization_barrier((x, earlier))[0]


def swap(x, size, shift):
    return lax.ppermute(x, "node", [(i, i ^ shift) for i in range(size)])


def within(pieces, size):
    return [pieces[0]] + [swap(pieces[s], size, s) for s in range(1, SET)]


def local(size, nodes, pair_nodes, prod_left, prod_right, prod_flag, prod_diag):
    place = lax.axis_index("node").astype(jnp.int32).reshape(1)
    order = nodes.shape[3]
    widths = [order * share // sum(SHARES) for share in SHARES]
    across = [list(range(i, size, SET)) for i in range(SET)]
    table = route(place, pair_nodes, prod_left, prod_right, prod_flag, prod_diag)
    own = exchange(pick(table, nodes, 0, 0, order))
    pieces = within(pick_sets(table, place, nodes, 2), size)
    other = swap(own, size, 1)
    middle = exchange(after(pick(table, nodes, 1, 0, order), (own, pieces[2])))
    left = left_pair(table, place, own, other)
    sents = regroup(pieces, widths)
    left_middle = product(left, middle)
    done, wholes, rests = (middle, left), [], []
    for j, sent in enumerate(sents):
        last = exchange(after(sent, done), across)
        done = (last, left_middle)
        if wholes:
            last = after(last, sums)
        panels = within(panels_of(place, left_middle, last), size)
        if wholes:
            panels = after(panels, wholes[-1])
        sums, rest = sums_of(table, place, panels, j < len(sents) - 1)
        rests.append(rest)
        if j < len(sents) - 1:
            wholes.append(exchange(sums[0], across))
    sums = [x if e == 0 else swap(x, size, SET * e) for e, x in enumerate(sums)]

    def move(rests):
        return [exchange(rest, across) for rest in rests]

    rests = lax.cond(table[8, 0] < SET, lambda rests: rests, move, rests)
    return diagrams_of(table, place, wholes, rests, sums)


def solution(mesh):
    placed = (P("grp", None, "node", None), P(), P(), P(), P(), P())
    return jax.shard_map(
        functools.partial(local, mesh.shape["node"]),
        mesh=mesh,
        in_specs=placed,
        out_specs=P("grp", None, "node", None),
        check_vma=False,
    )
```
